512 devices in a mesh: blk: 64 (over y, z_lo, core), row: 8 (over z_hi, x).
Axes of the slice: x: 4, y: 8, z: 8 (z_hi: 2, z_lo: 4; z = z_hi * 4 + z_lo), core: 2. Of those that a mesh axis runs over, the one named last changes fastest.
Arguments:
- features: float32 [32, 393216], P(None, ('blk', 'row')), may hold values from -6 to 6
- probes: bfloat16 [8, 393216], P(None, ('blk', 'row')), may hold values from -5 to 5
- inverse_scales: float32 [32], replicated, may hold values from 0.02 to 0.2
- round_index: int32 [1], replicated, may hold values from 1 to 31
- pivots: int32 [128], replicated, may hold values from 0 to 393215
Outputs:
- product: float32 [8, 393216], P(None, ('blk', 'row'))
- projection: float32 [8, 128], replicated
- quadratic: float32 [8], replicated
The draws below stay inside these ranges and needn't reach their ends.
Inputs may be any that keep to these rules, and one draw needn't show every extreme that they name: `pivots`: indices may repeat.
All inputs are finite; a program needn't handle non-finite values.
Results may differ from the reference program's by a relative error of at most 0.034.
Values may be sent and summed in bfloat16 or wider, within the bound.
No kernel may reach another device: no remote copies, remote signals or barrier semaphores. Data moves between devices by JAX's collectives and lax.ppermute only.
A program may use at most 64 MiB of HBM per device.

```python
import math
import jax
import jax.numpy as jnp
from jax import lax

FEAT = 32
PROBES = 8
RANK = 128
ROWS_DEV = 768
BLOCK = 6144
POINTS = 393216
N_BLK = 64
N_ROW = 8


def with_ends(entries, own_key, smallest, largest):
    index_at = [jax.random.randint(jax.random.fold_in(own_key, axis), (), 0, length) for axis, length in enumerate(entries.shape)]
    main_axis = entries.shape.index(max(entries.shape))
    neighbour = index_at[:main_axis] + [(index_at[main_axis] + 1) % entries.shape[main_axis]] + index_at[main_axis + 1:]
    return entries.at[tuple(index_at)].set(smallest).at[tuple(neighbour)].set(largest)


def shard_levels(key, extent, shards, low, largest):
    def one(position, parts):
        heights = jax.random.uniform(jax.random.fold_in(jax.random.fold_in(key, 6), position), (parts,), jnp.float32, low / len(shards), largest / len(shards))
        return jnp.repeat(jnp.exp(heights), extent[position] // parts).reshape((-1,) + (1,) * (len(extent) - position - 1))

    gain = one(*shards[0])
    for cut in shards[1:]:
        gain = gain * one(*cut)
    return gain


def scatter_about(rng, shape, scale, most, split=(), kind=jnp.bfloat16):
    drawn = jax.random.normal(rng, shape, jnp.float32) * scale
    if len(split) > 0:
        drawn = shard_levels(rng, shape, split, -0.22, 0.18) * drawn
    return jnp.clip(drawn, min=-most, max=most).astype(kind)


def setup_inputs(seed: int = 0) -> dict:
    streams_of = jax.random.split(jax.random.key(seed), 6)
    return {
        "features": scatter_about(streams_of[0], (FEAT, POINTS), 1.0, 6.0, ((1, 512),), jnp.float32),
        "probes": scatter_about(streams_of[1], (PROBES, POINTS), 1.0, 5.0, ((1, 512),)),
        "inverse_scales": jnp.clip(jnp.exp(jax.random.uniform(streams_of[2], (FEAT,), jnp.float32, math.log(0.02), math.log(0.2))), 0.02, 0.2),
        "round_index": jax.random.randint(streams_of[3], (1,), 1, N_BLK // 2).astype(jnp.int32),
        "pivots": with_ends(jax.random.randint(streams_of[4], (RANK,), 0, POINTS), jax.random.fold_in(streams_of[4], 1), 0, POINTS - 1).astype(jnp.int32),
    }


def square_norm(scaled_feat):
    wide = scaled_feat.astype(jnp.float32)
    return lax.optimization_barrier(jnp.sum(wide * wide, axis=0))

def kernel_block(row_feat, row_norm, col_feat, col_norm):
    inner_prod = jnp.dot(row_feat.T, col_feat, preferred_element_type=jnp.float32)
    distance = row_norm[:, None] + col_norm[None, :] - 2.0 * inner_prod
    return jnp.exp(-0.5 * distance).astype(jnp.bfloat16)

def reference(features, probes, inverse_scales, round_index, pivots):
    scaled = (features * jnp.sqrt(inverse_scales)[:, None]).astype(jnp.bfloat16)
    norms = square_norm(scaled)
    round_shift = round_index[0]
    scaled_groups = scaled.reshape(FEAT, N_BLK, BLOCK).transpose(1, 0, 2)
    probe_groups = probes.reshape(PROBES, N_BLK, BLOCK).transpose(1, 0, 2)
    norm_groups = norms.reshape(N_BLK, BLOCK)

    def group_terms(group):
        partner = (group + round_shift) % N_BLK
        col_feat = scaled_groups[partner]
        col_norm = norm_groups[partner]
        col_probe = probe_groups[partner]
        own_feat = scaled_groups[group]
        own_norm = norm_groups[group]
        own_probe = probe_groups[group]

        def row_slab(slab):
            first_row = (slab * ROWS_DEV).astype(jnp.int32)
            row_feat = lax.dynamic_slice_in_dim(own_feat, first_row, ROWS_DEV, 1)
            row_norm = lax.dynamic_slice_in_dim(own_norm, first_row, ROWS_DEV, 0)
            row_probe = lax.dynamic_slice_in_dim(own_probe, first_row, ROWS_DEV, 1)
            kernel = kernel_block(row_feat, row_norm, col_feat, col_norm)
            front = jnp.dot(col_probe, kernel.T, preferred_element_type=jnp.float32)
            back_part = jnp.dot(row_probe, kernel, preferred_element_type=jnp.float32)
            return (front, back_part)
        fronts, back_terms = lax.map(row_slab, jnp.arange(N_ROW, dtype=jnp.int32))
        front_all = fronts.transpose(1, 0, 2).reshape(PROBES, BLOCK)
        return (front_all, lax.optimization_barrier(jnp.sum(back_terms, axis=0)))
    forward, backward = lax.map(group_terms, jnp.arange(N_BLK, dtype=jnp.int32))
    backward = jnp.roll(backward, round_shift, axis=0)
    product_groups = 8.0 / math.sqrt(BLOCK) * (forward + backward)
    product = product_groups.transpose(1, 0, 2).reshape(PROBES, POINTS)
    pivot_feat = scaled[:, pivots]
    pivot_norm = square_norm(pivot_feat)

    def pivot_terms(group):
        kernel = kernel_block(scaled_groups[group], norm_groups[group], pivot_feat, pivot_norm)
        return jnp.dot(probe_groups[group], kernel, preferred_element_type=jnp.float32)
    projection = lax.optimization_barrier(jnp.sum(lax.map(pivot_terms, jnp.arange(N_BLK, dtype=jnp.int32)), axis=0))
    projection = projection * (8.0 / math.sqrt(POINTS))
    quadratic = lax.optimization_barrier(jnp.sum(probes.astype(jnp.float32) * product, axis=1)) / math.sqrt(POINTS)
    return (product, projection, quadratic)
```

```python
import math

import jax
import jax.numpy as jnp
from jax import lax
from jax.sharding import Mesh
from jax.sharding import PartitionSpec as P

Y, ZLO, CORE, ZHI, X = 8, 4, 2, 2, 4
GROUP_AXES = ("y", "zlo", "core")
ALL_AXES = ("y", "zlo", "core", "zhi", "x")
MAX_SHIFT = 31


def shifted(x, axes, by):
    peers = lax.axis_size(axes)
    return lax.ppermute(x, axes, [(i, (i + by) % peers) for i in range(peers)])


def gathered(x, axes):
    peers = lax.axis_size(axes)
    return lax.all_to_all(jnp.broadcast_to(x[None], (peers,) + x.shape), axes, 0, 0)


def square_norm(scaled_feat):
    wide = scaled_feat.astype(jnp.float32)
    return jnp.sum(wide * wide, axis=0)


def kernel_block(row_feat, row_norm, col_feat, col_norm):
    inner_prod = jnp.dot(row_feat.T, col_feat, preferred_element_type=jnp.float32)
    distance = row_norm[:, None] + col_norm[None, :] - 2.0 * inner_prod
    return jnp.exp(-0.5 * distance).astype(jnp.bfloat16)


def body(features, probes, inverse_scales, round_index, pivots):
    feat_count, row_count = features.shape
    group_count = lax.axis_size(GROUP_AXES)
    row_devices = lax.axis_size(("zhi", "x"))
    block_points = row_count * row_devices
    total_points = block_points * group_count

    scaled = (features * jnp.sqrt(inverse_scales)[:, None]).astype(jnp.bfloat16)
    packed = jnp.concatenate([scaled, probes], axis=0)

    first_point = lax.axis_index(ALL_AXES) * row_count
    points = first_point + jnp.arange(row_count, dtype=jnp.int32)
    pivot_mask = (points[:, None] == pivots[None, :]).astype(jnp.bfloat16)
    pivot_part = jnp.dot(scaled, pivot_mask, preferred_element_type=jnp.float32).astype(jnp.bfloat16)
    pivot_some = jnp.sum(gathered(pivot_part, ("y", "x")), axis=0)

    def both_ways(shift):
        def branch(data):
            return shifted(data, GROUP_AXES, -shift), shifted(data, GROUP_AXES, shift)

        return branch

    after, before = lax.switch(
        round_index[0] - 1, [both_ways(k) for k in range(1, MAX_SHIFT + 1)], packed
    )
    paired = shifted(packed, ("zhi",), 1)
    pivot_feat = jnp.sum(gathered(pivot_some, ("zlo", "core", "zhi")), axis=0)
    cols = gathered(jnp.stack([after, before]), ("x",)).reshape(-1, packed.shape[0], row_count)

    own_norm = square_norm(scaled)
    pivot_kernel = kernel_block(scaled, own_norm, pivot_feat, square_norm(pivot_feat))
    projection_part = jnp.dot(probes, pivot_kernel, preferred_element_type=jnp.float32)

    rows = jnp.concatenate([packed, paired], axis=1)
    row_feat = rows[:feat_count]
    row_probe = rows[feat_count:]
    row_norm = square_norm(row_feat)
    total = jnp.zeros((probes.shape[0], rows.shape[1]), jnp.float32)
    for piece in range(cols.shape[0]):
        col_feat = cols[piece, :feat_count]
        col_probe = cols[piece, feat_count:]
        kernel = kernel_block(col_feat, square_norm(col_feat), row_feat, row_norm)
        total = total + jnp.dot(col_probe, kernel, preferred_element_type=jnp.float32)

    total = 8.0 / math.sqrt(block_points) * total
    product = total[:, :row_count] + shifted(total[:, row_count:], ("zhi",), 1)
    quadratic_part = jnp.sum(row_probe.astype(jnp.float32) * total, axis=1)
    sums = jnp.concatenate(
        [projection_part, jnp.broadcast_to(quadratic_part[:, None], projection_part.shape)], axis=1
    )
    sums = jnp.sum(gathered(sums, ("y", "x")), axis=0)
    sums = jnp.sum(gathered(sums, ("zlo", "core", "zhi")), axis=0)
    rank = projection_part.shape[1]
    projection = sums[:, :rank] * (8.0 / math.sqrt(total_points))
    quadratic = sums[:, rank] / math.sqrt(total_points)
    return product, projection, quadratic


def solution(mesh):
    fine = Mesh(mesh.devices.reshape(Y, ZLO, CORE, ZHI, X), ALL_AXES)
    split = P(None, ALL_AXES)
    return jax.shard_map(
        body,
        mesh=fine,
        in_specs=(split, split, P(), P(), P()),
        out_specs=(split, P(), P()),
        check_vma=False,
    )
```

```python
import math

import jax
import jax.numpy as jnp
from jax import lax
from jax.sharding import Mesh
from jax.sharding import PartitionSpec as P

Y, ZLO, CORE, ZHI, X = 8, 4, 2, 2, 4
GROUP_AXES = ("y", "zlo", "core")
ALL_AXES = ("y", "zlo", "core", "zhi", "x")
SUM_AXES = (("y", "core"), ("zlo", "zhi", "x"))
MAX_SHIFT = 31


def crossed(x, axis, bit):
    return lax.ppermute(x, axis, [(i, i ^ bit) for i in range(lax.axis_size(axis))])


def gathered(x, axes):
    peers = lax.axis_size(axes)
    return lax.all_to_all(jnp.broadcast_to(x[None], (peers,) + x.shape), axes, 0, 0)


def from_partner(x, shift):
    groups, halves, width = lax.axis_size(GROUP_AXES), lax.axis_size("zhi"), lax.axis_size("x")
    pairs = []
    for group in range(groups):
        for half in range(halves):
            for place in range(width):
                way = 1 - 2 * ((place + group) % 2)
                source = (group + way * shift) % groups
                source = (source * halves + (half ^ place // 2)) * width + place
                pairs.append((source, (group * halves + half) * width + place))
    return lax.ppermute(x, ALL_AXES, pairs)


def square_norm(scaled_feat):
    wide = scaled_feat.astype(jnp.float32)
    return jnp.sum(wide * wide, axis=0)


def kernel_block(row_feat, row_norm, col_feat, col_norm):
    inner_prod = jnp.dot(row_feat.T, col_feat, preferred_element_type=jnp.float32)
    distance = row_norm[:, None] + col_norm[None, :] - 2.0 * inner_prod
    return jnp.exp(-0.5 * distance).astype(jnp.bfloat16)


def body(features, probes, inverse_scales, round_index, pivots):
    feat_count, row_count = features.shape
    probe_count = probes.shape[0]
    rank = pivots.shape[0]
    width = lax.axis_size("x")
    group_count = lax.axis_size(GROUP_AXES)
    block_points = row_count * lax.axis_size(("zhi", "x"))
    total_points = block_points * group_count
    product_scale = 8.0 / math.sqrt(block_points)

    scaled = (features * jnp.sqrt(inverse_scales)[:, None]).astype(jnp.bfloat16)
    packed = jnp.concatenate([scaled, probes], axis=0)
    quad = gathered(packed, "x")

    first_point = lax.axis_index(ALL_AXES) * row_count
    points = first_point + jnp.arange(row_count, dtype=jnp.int32)
    pivot_mask = (points[:, None] == pivots[None, :]).astype(jnp.bfloat16)
    pivot_part = jnp.dot(scaled, pivot_mask, preferred_element_type=jnp.float32).astype(jnp.bfloat16)

    def fetch(shift):
        def branch(data, part):
            some = jnp.sum(gathered(part, SUM_AXES[0]), axis=0)
            return from_partner(data, shift), some

        return branch

    pieces, pivot_some = lax.switch(
        round_index[0] - 1, [fetch(k) for k in range(1, MAX_SHIFT + 1)], quad, pivot_part
    )
    pivot_feat = jnp.sum(gathered(pivot_some, SUM_AXES[1]), axis=0)
    own_norm = square_norm(scaled)
    pivot_kernel = kernel_block(scaled, own_norm, pivot_feat, square_norm(pivot_feat))
    projection_part = jnp.dot(probes, pivot_kernel, preferred_element_type=jnp.float32)

    rows = quad.transpose(1, 0, 2).reshape(-1, width * row_count)
    row_feat = rows[:feat_count]
    row_probe = rows[feat_count:]
    row_norm = square_norm(row_feat)
    total = jnp.zeros((probe_count, width * row_count), jnp.float32)
    for place in range(width):
        col_feat = pieces[place, :feat_count]
        col_probe = pieces[place, feat_count:]
        kernel = kernel_block(col_feat, square_norm(col_feat), row_feat, row_norm)
        total = total + jnp.dot(col_probe, kernel, preferred_element_type=jnp.float32)
    total = product_scale * total
    quadratic_part = jnp.sum(row_probe.astype(jnp.float32) * total, axis=1)

    place = lax.axis_index("x")
    halves = total.reshape(probe_count, 2, 2 * row_count)
    kept = lax.dynamic_index_in_dim(halves, place // 2, 1, keepdims=False)
    given = lax.dynamic_index_in_dim(halves, 1 - place // 2, 1, keepdims=False)
    kept = kept + crossed(given, "x", 2)
    parts = kept.reshape(probe_count, 2, row_count)
    kept = lax.dynamic_index_in_dim(parts, place % 2, 1, keepdims=False)
    given = lax.dynamic_index_in_dim(parts, 1 - place % 2, 1, keepdims=False)
    product = kept + crossed(given, "x", 1)

    sums = jnp.concatenate(
        [projection_part, jnp.broadcast_to(quadratic_part[:, None], projection_part.shape)], axis=1
    )
    sums = jnp.sum(gathered(sums, SUM_AXES[0]), axis=0)
    sums = jnp.sum(gathered(sums, SUM_AXES[1]), axis=0)
    projection = sums[:, :rank] * (8.0 / math.sqrt(total_points))
    quadratic = sums[:, rank] / math.sqrt(total_points)
    return product, projection, quadratic


def solution(mesh):
    fine = Mesh(mesh.devices.reshape(Y, ZLO, CORE, ZHI, X), ALL_AXES)
    split = P(None, ALL_AXES)
    return jax.shard_map(
        body,
        mesh=fine,
        in_specs=(split, split, P(), P(), P()),
        out_specs=(split, P(), P()),
        check_vma=False,
    )
```

```python
import functools
import math

import jax
import jax.numpy as jnp
from jax import lax
from jax.experimental import pallas as pl
from jax.experimental.pallas import tpu as pltpu
from jax.sharding import Mesh
from jax.sharding import PartitionSpec as P

Y, ZLO, CORE, ZHI, X = 8, 4, 2, 2, 4
GROUP_AXES = ("y", "zlo", "core")
ALL_AXES = ("y", "zlo", "core", "zhi", "x")
FIRST_SUM, SECOND_SUM = ("y", "core"), ("zlo", "zhi")
MAX_SHIFT = 31
EXTRA = 16
VMEM_LIMIT = 48 * 2**20


def size_of(axes):
    return lax.axis_size(axes)


def exchanged(x, axes):
    return lax.all_to_all(x, axes, 0, 0)


def from_partner(x, shift):
    groups, halves, width = size_of(GROUP_AXES), size_of("zhi"), size_of("x")
    pairs = []
    for group in range(groups):
        for half in range(halves):
            for place in range(width):
                way = 1 - 2 * ((place + group) % 2)
                source = (group + way * shift) % groups
                source = (source * halves + (half ^ place // 2)) * width + place
                pairs.append((source, (group * halves + half) * width + place))
    return lax.ppermute(x, ALL_AXES, pairs)


def local(
    kernel, name, out_shape, *args, scalars=0, flops=0, exps=0, scratch=(), space=pltpu.VMEM, room=VMEM_LIMIT
):
    moved = sum(math.prod(a.shape) * a.dtype.itemsize for a in args)
    specs = [pl.BlockSpec(memory_space=pltpu.SMEM)] * scalars
    specs += [pl.BlockSpec(memory_space=space)] * (len(args) - scalars)
    return pl.pallas_call(
        kernel,
        name=name,
        out_shape=out_shape,
        in_specs=specs,
        out_specs=jax.tree.map(lambda _: pl.BlockSpec(memory_space=pltpu.VMEM), out_shape),
        scratch_shapes=scratch,
        cost_estimate=pl.CostEstimate(flops=flops, bytes_accessed=moved, transcendentals=exps),
        compiler_params=pltpu.CompilerParams(vmem_limit_bytes=room),
    )(*args)


def extended(feat, ones_first):
    wide = feat.astype(jnp.float32)
    half = -0.5 * jnp.sum(wide * wide, axis=0, keepdims=True)
    high = half.astype(jnp.bfloat16).astype(jnp.float32)
    middle = (half - high).astype(jnp.bfloat16).astype(jnp.float32)
    low = half - high - middle
    row = lax.broadcasted_iota(jnp.int32, (EXTRA, feat.shape[1]), 0)
    ones, norm = (0, 3) if ones_first else (3, 0)
    rest = jnp.where((row >= ones) & (row < ones + 3), 1.0, 0.0)
    for offset, piece in enumerate((high, middle, low)):
        rest = jnp.where(row == norm + offset, piece, rest)
    return jnp.concatenate([feat, rest.astype(jnp.bfloat16)], axis=0)


def turned(x):
    return x.astype(jnp.float32).T.astype(jnp.bfloat16)


def prepare_kernel(feat_hbm, scale_hbm, probe_hbm, out_ref, feat_ref, scale_ref, probe_ref, done):
    copies = [
        pltpu.make_async_copy(source, target, done.at[index])
        for index, (source, target) in enumerate(
            ((feat_hbm, feat_ref), (scale_hbm, scale_ref), (probe_hbm, probe_ref))
        )
    ]
    for copy in copies:
        copy.start()
    for copy in copies:
        copy.wait()
    count = feat_ref.shape[0]
    row = lax.broadcasted_iota(jnp.int32, (count, count), 0)
    col = lax.broadcasted_iota(jnp.int32, (count, count), 1)
    spread = jnp.broadcast_to(scale_ref[...], (count, count))
    scale = jnp.sum(jnp.where(row == col, spread, 0.0), axis=1, keepdims=True)
    scaled = (feat_ref[...] * jnp.sqrt(scale)).astype(jnp.bfloat16)
    packed = jnp.concatenate([scaled, probe_ref[...]], axis=0)
    for copy in range(out_ref.shape[0]):
        out_ref[copy] = packed


def own_pivots_kernel(first_ref, packed_ref, pivot_ref, out_ref):
    count, rank = out_ref.shape
    points = packed_ref.shape[2]
    point = lax.broadcasted_iota(jnp.int32, (points, rank), 0) + first_ref[0]
    mask = jnp.where(point == pivot_ref[...], 1.0, 0.0).astype(jnp.bfloat16)
    part = jnp.dot(packed_ref[0, :count], mask, preferred_element_type=jnp.float32)
    out_ref[...] = part.astype(jnp.bfloat16)


def sum_spread_kernel(in_ref, out_ref):
    total = in_ref[0].astype(jnp.float32)
    for peer in range(1, in_ref.shape[0]):
        total = total + in_ref[peer].astype(jnp.float32)
    for copy in range(out_ref.shape[0]):
        out_ref[copy] = total.astype(out_ref.dtype)


def product_kernel(row_ref, col_ref, sum_ref, quad_ref, row_all, col_all, *, count, scale):
    width, probes = row_ref.shape[0], sum_ref.shape[1]
    for place in range(width):
        row_all[place] = extended(row_ref[place, :count], True)
        col_all[place] = turned(extended(col_ref[place, :count], False))

    def step(place, quad):
        total = jnp.zeros(sum_ref.shape[1:], jnp.float32)
        for other in range(width):
            power = jnp.dot(col_all[other], row_all[place], preferred_element_type=jnp.float32)
            kernel = jnp.exp(power).astype(jnp.bfloat16)
            col_probe = col_ref[other, count : count + probes]
            total = total + jnp.dot(col_probe, kernel, preferred_element_type=jnp.float32)
        total = scale * total
        sum_ref[place] = total
        row_probe = row_ref[place, count : count + probes].astype(jnp.float32)
        return quad + jnp.sum(row_probe * total, axis=1, keepdims=True)

    quad = lax.fori_loop(0, width, step, jnp.zeros((probes, 1), jnp.float32))
    quad_ref[...] = jnp.broadcast_to(quad, quad_ref.shape)


def projection_kernel(pivot_ref, here_ref, row_ref, sum_ref, quad_ref, out_ref, *, count):
    width, probes, points = sum_ref.shape
    rank = pivot_ref.shape[2]
    pivot = pivot_ref[0].astype(jnp.float32)
    for peer in range(1, pivot_ref.shape[0]):
        pivot = pivot + pivot_ref[peer].astype(jnp.float32)
    pivot = turned(extended(pivot.astype(jnp.bfloat16), False))
    total = jnp.zeros((probes, rank), jnp.float32)
    for place in range(width):
        row = extended(row_ref[place, :count], True)
        power = jnp.dot(pivot, row, preferred_element_type=jnp.float32)
        kernel = jnp.exp(power).astype(jnp.bfloat16)
        total = total + lax.dot_general(
            row_ref[place, count : count + probes],
            kernel,
            (((1,), (1,)), ((), ())),
            preferred_element_type=jnp.float32,
        )
    total = jnp.where(here_ref[...] != 0, total, 0.0)
    for place in range(width):
        out_ref[place, :, :points] = sum_ref[place]
        out_ref[place, :, points : points + rank] = total
        out_ref[place, :, points + rank :] = quad_ref[...]


def own_sums_kernel(in_ref, product_ref, out_ref):
    probes, points = product_ref.shape
    total = in_ref[0]
    for peer in range(1, in_ref.shape[0]):
        total = total + in_ref[peer]
    product_ref[...] = total[:, :points]
    rank = (total.shape[1] - points) // 2
    rows = [total[probe : probe + 1, points : points + rank] for probe in range(probes)]
    row = lax.broadcasted_iota(jnp.int32, (probes, rank), 0)
    lane = lax.broadcasted_iota(jnp.int32, (probes, rank), 1)
    last = jnp.where(row == lane, total[:, points + rank :], 0.0)
    rows.append(jnp.sum(last, axis=0, keepdims=True))
    packed = jnp.concatenate(rows, axis=1)
    for copy in range(out_ref.shape[0]):
        out_ref[copy] = packed


def body(features, probes, inverse_scales, round_index, pivots):
    count, row_count = features.shape
    probe_count, rank = probes.shape[0], pivots.shape[0]
    rows = count + probe_count
    width = size_of("x")
    block_points = row_count * size_of(("zhi", "x"))
    total_points = block_points * size_of(GROUP_AXES)
    shape = jax.ShapeDtypeStruct

    packed = local(
        prepare_kernel,
        "prepare",
        shape((width, rows, row_count), jnp.bfloat16),
        features,
        inverse_scales.reshape(1, count),
        probes,
        scratch=(
            pltpu.VMEM(features.shape, features.dtype),
            pltpu.VMEM((1, count), inverse_scales.dtype),
            pltpu.VMEM(probes.shape, probes.dtype),
            pltpu.SemaphoreType.DMA((3,)),
        ),
        space=pltpu.HBM,
        room=60 * 2**20,
    )
    quad = exchanged(packed, "x")

    first_point = (lax.axis_index(ALL_AXES) * row_count).astype(jnp.int32)
    pivot_row = pivots.reshape(1, rank)
    pivot_part = local(
        own_pivots_kernel,
        "own_pivots",
        shape((count, rank), jnp.bfloat16),
        first_point.reshape(1),
        packed,
        pivot_row,
        scalars=1,
        flops=2 * count * row_count * rank,
    )
    pivot_here = (pivot_row // row_count % width == lax.axis_index("x")).astype(jnp.int32)

    def fetch(shift):
        def branch(data, part):
            spread = jnp.broadcast_to(part[None], (size_of(FIRST_SUM),) + part.shape)
            some = jnp.sum(exchanged(spread, FIRST_SUM), axis=0)
            pieces = lax.optimization_barrier(from_partner(data, shift))
            return pieces, some

        return branch

    pieces, pivot_some = lax.switch(
        round_index[0] - 1, [fetch(k) for k in range(1, MAX_SHIFT + 1)], quad, pivot_part
    )
    spread = jnp.broadcast_to(pivot_some[None], (size_of(SECOND_SUM), count, rank))
    pivot_all = exchanged(spread, SECOND_SUM)

    sums, quadratic_part = local(
        functools.partial(
            product_kernel, count=count, scale=8.0 / math.sqrt(block_points)
        ),
        "products",
        (
            shape((width, probe_count, row_count), jnp.float32),
            shape((probe_count, rank), jnp.float32),
        ),
        quad,
        pieces,
        flops=2 * (width * row_count) ** 2 * (count + EXTRA + probe_count),
        exps=(width * row_count) ** 2,
        scratch=(
            pltpu.VMEM((width, count + EXTRA, row_count), jnp.bfloat16),
            pltpu.VMEM((width, row_count, count + EXTRA), jnp.bfloat16),
        ),
    )
    parts = local(
        functools.partial(projection_kernel, count=count),
        "projection",
        shape((width, probe_count, row_count + 2 * rank), jnp.float32),
        pivot_all,
        pivot_here,
        quad,
        sums,
        quadratic_part,
        flops=2 * width * row_count * rank * (count + EXTRA + probe_count),
        exps=width * row_count * rank,
    )

    packed_sums = (probe_count + 1) * rank
    product, spread = local(
        own_sums_kernel,
        "own_sums",
        (
            shape((probe_count, row_count), jnp.float32),
            shape((size_of(FIRST_SUM), 1, packed_sums), jnp.float32),
        ),
        exchanged(parts, "x"),
    )
    spread = local(
        sum_spread_kernel,
        "first_sum",
        shape((size_of(SECOND_SUM), 1, packed_sums), jnp.float32),
        exchanged(spread, FIRST_SUM),
    )
    total = jnp.sum(exchanged(spread, SECOND_SUM), axis=(0, 1)) / math.sqrt(total_points)
    projection = 8.0 * total[: probe_count * rank].reshape(probe_count, rank)
    quadratic = total[probe_count * rank : probe_count * rank + probe_count]
    return product, projection, quadratic


def solution(mesh):
    fine = Mesh(mesh.devices.reshape(Y, ZLO, CORE, ZHI, X), ALL_AXES)
    split = P(None, ALL_AXES)
    return jax.shard_map(
        body,
        mesh=fine,
        in_specs=(split, split, P(), P(), P()),
        out_specs=(split, P(), P()),
        check_vma=False,
    )
```

```python
import functools
import math

import jax
import jax.numpy as jnp
from jax import lax
from jax.experimental import pallas as pl
from jax.experimental.pallas import tpu as pltpu
from jax.sharding import Mesh
from jax.sharding import PartitionSpec as P

Y, ZLO, CORE, ZHI, X = 8, 4, 2, 2, 4
GROUP_AXES = ("y", "zlo", "core")
ALL_AXES = ("y", "zlo", "core", "zhi", "x")
FIRST_SUM, SECOND_SUM = ("y", "core"), ("zlo", "zhi")
MAX_SHIFT = 31
EXTRA = 16
VMEM_LIMIT = 48 * 2**20


def size_of(axes):
    return lax.axis_size(axes)


def exchanged(x, axes):
    return lax.all_to_all(x, axes, 0, 0)


def from_partner(x, shift):
    groups, halves, width = size_of(GROUP_AXES), size_of("zhi"), size_of("x")
    pairs = []
    for group in range(groups):
        for half in range(halves):
            for place in range(width):
                way = 1 - 2 * ((place + group) % 2)
                source = (group + way * shift) % groups
                source = (source * halves + (half ^ place // 2)) * width + place
                pairs.append((source, (group * halves + half) * width + place))
    return lax.ppermute(x, ALL_AXES, pairs)


def local(
    kernel, name, out_shape, *args, scalars=0, flops=0, exps=0, scratch=(), space=pltpu.VMEM, room=VMEM_LIMIT
):
    moved = sum(math.prod(a.shape) * a.dtype.itemsize for a in args)
    specs = [pl.BlockSpec(memory_space=pltpu.SMEM)] * scalars
    specs += [pl.BlockSpec(memory_space=space)] * (len(args) - scalars)
    return pl.pallas_call(
        kernel,
        name=name,
        out_shape=out_shape,
        in_specs=specs,
        out_specs=jax.tree.map(lambda _: pl.BlockSpec(memory_space=pltpu.VMEM), out_shape),
        scratch_shapes=scratch,
        cost_estimate=pl.CostEstimate(flops=flops, bytes_accessed=moved, transcendentals=exps),
        compiler_params=pltpu.CompilerParams(vmem_limit_bytes=room),
    )(*args)


def extended(feat, ones_first):
    wide = feat.astype(jnp.float32)
    half = -0.5 * jnp.sum(wide * wide, axis=0, keepdims=True)
    high = half.astype(jnp.bfloat16).astype(jnp.float32)
    middle = (half - high).astype(jnp.bfloat16).astype(jnp.float32)
    low = half - high - middle
    row = lax.broadcasted_iota(jnp.int32, (EXTRA, feat.shape[1]), 0)
    ones, norm = (0, 3) if ones_first else (3, 0)
    rest = jnp.where((row >= ones) & (row < ones + 3), 1.0, 0.0)
    for offset, piece in enumerate((high, middle, low)):
        rest = jnp.where(row == norm + offset, piece, rest)
    return jnp.concatenate([feat, rest.astype(jnp.bfloat16)], axis=0)


def turned(x):
    return x.astype(jnp.float32).T.astype(jnp.bfloat16)


def prepare_kernel(feat_hbm, scale_hbm, probe_hbm, out_ref, feat_ref, scale_ref, probe_ref, done):
    copies = [
        pltpu.make_async_copy(source, target, done.at[index])
        for index, (source, target) in enumerate(
            ((feat_hbm, feat_ref), (scale_hbm, scale_ref), (probe_hbm, probe_ref))
        )
    ]
    for copy in copies:
        copy.start()
    for copy in copies:
        copy.wait()
    count = feat_ref.shape[0]
    row = lax.broadcasted_iota(jnp.int32, (count, count), 0)
    col = lax.broadcasted_iota(jnp.int32, (count, count), 1)
    spread = jnp.broadcast_to(scale_ref[...], (count, count))
    scale = jnp.sum(jnp.where(row == col, spread, 0.0), axis=1, keepdims=True)
    scaled = (feat_ref[...] * jnp.sqrt(scale)).astype(jnp.bfloat16)
    packed = jnp.concatenate([scaled, probe_ref[...]], axis=0)
    for copy in range(out_ref.shape[0]):
        out_ref[copy] = packed


def own_pivots_kernel(first_ref, packed_ref, pivot_ref, out_ref):
    count, rank = out_ref.shape
    points = packed_ref.shape[2]
    point = lax.broadcasted_iota(jnp.int32, (points, rank), 0) + first_ref[0]
    mask = jnp.where(point == pivot_ref[...], 1.0, 0.0).astype(jnp.bfloat16)
    part = jnp.dot(packed_ref[0, :count], mask, preferred_element_type=jnp.float32)
    out_ref[...] = part.astype(jnp.bfloat16)


def sum_spread_kernel(in_ref, out_ref):
    total = in_ref[0].astype(jnp.float32)
    for peer in range(1, in_ref.shape[0]):
        total = total + in_ref[peer].astype(jnp.float32)
    for copy in range(out_ref.shape[0]):
        out_ref[copy] = total.astype(out_ref.dtype)


def pair_sum(row_all, col_all, col_ref, place, other, count, probes):
    power = jnp.dot(col_all[other], row_all[place], preferred_element_type=jnp.float32)
    kernel = jnp.exp(power).astype(jnp.bfloat16)
    col_probe = col_ref[other, count : count + probes]
    return jnp.dot(col_probe, kernel, preferred_element_type=jnp.float32)


def first_half_kernel(
    ahead_ref, row_ref, col_ref, sum_ref, quad_ref, row_all, col_all, *, count, scale
):
    width, probes = row_ref.shape[0], sum_ref.shape[1]
    ahead = ahead_ref[0] == 1
    for place in range(width):
        row_all[place] = extended(row_ref[place, :count], True)
        col_all[place] = turned(extended(col_ref[place, :count], False))
    sum_ref[...] = jnp.zeros_like(sum_ref)

    def step(turn, carry):
        for part in range(4):
            place = jnp.where(ahead, 2 * turn + part // 2, 2 + turn)
            other = jnp.where(ahead, part % 2, part)
            sum_ref[place] += pair_sum(row_all, col_all, col_ref, place, other, count, probes)
        return carry

    lax.fori_loop(0, 2, step, 0)
    quad = jnp.zeros((probes, 1), jnp.float32)
    for place in range(width):
        row_probe = row_ref[place, count : count + probes].astype(jnp.float32)
        quad = quad + jnp.sum(row_probe * sum_ref[place], axis=1, keepdims=True)
    quad_ref[...] = jnp.broadcast_to(scale * quad, quad_ref.shape)


def second_half_kernel(
    ahead_ref, row_all, col_all, col_ref, first_ref, sum_ref, *, count, scale
):
    width, probes = first_ref.shape[:2]
    ahead = ahead_ref[0] == 1
    sum_ref[...] = first_ref[...]

    def step(turn, carry):
        for part in range(4):
            place = jnp.where(ahead, 2 * turn + part // 2, turn)
            other = jnp.where(ahead, 2 + part % 2, part)
            sum_ref[place] += pair_sum(row_all, col_all, col_ref, place, other, count, probes)
        return carry

    lax.fori_loop(0, 2, step, 0)
    for place in range(width):
        sum_ref[place] = scale * sum_ref[place]


def projection_kernel(pivot_ref, here_ref, row_ref, quad_ref, out_ref, *, count):
    width, rank = row_ref.shape[0], pivot_ref.shape[2]
    probes = quad_ref.shape[0]
    pivot = pivot_ref[0].astype(jnp.float32)
    for peer in range(1, pivot_ref.shape[0]):
        pivot = pivot + pivot_ref[peer].astype(jnp.float32)
    pivot = turned(extended(pivot.astype(jnp.bfloat16), False))
    total = jnp.zeros((probes, rank), jnp.float32)
    for place in range(width):
        row = extended(row_ref[place, :count], True)
        power = jnp.dot(pivot, row, preferred_element_type=jnp.float32)
        kernel = jnp.exp(power).astype(jnp.bfloat16)
        total = total + lax.dot_general(
            row_ref[place, count : count + probes],
            kernel,
            (((1,), (1,)), ((), ())),
            preferred_element_type=jnp.float32,
        )
    total = jnp.where(here_ref[...] != 0, total, 0.0)
    rows = [total[probe : probe + 1] for probe in range(probes)]
    row = lax.broadcasted_iota(jnp.int32, (probes, rank), 0)
    lane = lax.broadcasted_iota(jnp.int32, (probes, rank), 1)
    rows.append(jnp.sum(jnp.where(row == lane, quad_ref[...], 0.0), axis=0, keepdims=True))
    packed = jnp.concatenate(rows, axis=1)
    for copy in range(out_ref.shape[0]):
        out_ref[copy] = packed


def join_kernel(sum_ref, total_ref, out_ref):
    width, probes, points = sum_ref.shape
    rank = (out_ref.shape[2] - points) // 2
    total = total_ref[0]
    for peer in range(1, total_ref.shape[0]):
        total = total + total_ref[peer]
    rows = [total[:, probe * rank : (probe + 1) * rank] for probe in range(probes)]
    last = jnp.broadcast_to(total[:, probes * rank :], (probes, rank))
    joined = jnp.concatenate([jnp.concatenate(rows, axis=0), last], axis=1)
    for place in range(width):
        out_ref[place, :, :points] = sum_ref[place]
        out_ref[place, :, points:] = joined


def finish_kernel(in_ref, product_ref, projection_ref, quadratic_ref, *, projection_scale):
    probes, points = product_ref.shape
    rank = projection_ref.shape[1]
    total = in_ref[0]
    for peer in range(1, in_ref.shape[0]):
        total = total + in_ref[peer]
    product_ref[...] = total[:, :points]
    projection_ref[...] = projection_scale * total[:, points : points + rank]
    quadratic_ref[...] = total[0, points + rank : points + rank + probes]


def body(features, probes, inverse_scales, round_index, pivots):
    count, row_count = features.shape
    probe_count, rank = probes.shape[0], pivots.shape[0]
    rows = count + probe_count
    width = size_of("x")
    block_points = row_count * size_of(("zhi", "x"))
    total_points = block_points * size_of(GROUP_AXES)
    shape = jax.ShapeDtypeStruct

    packed = local(
        prepare_kernel,
        "prepare",
        shape((width, rows, row_count), jnp.bfloat16),
        features,
        inverse_scales.reshape(1, count),
        probes,
        scratch=(
            pltpu.VMEM(features.shape, features.dtype),
            pltpu.VMEM((1, count), inverse_scales.dtype),
            pltpu.VMEM(probes.shape, probes.dtype),
            pltpu.SemaphoreType.DMA((3,)),
        ),
        space=pltpu.HBM,
        room=60 * 2**20,
    )
    quad = exchanged(packed, "x")

    first_point = (lax.axis_index(ALL_AXES) * row_count).astype(jnp.int32)
    pivot_row = pivots.reshape(1, rank)
    pivot_part = local(
        own_pivots_kernel,
        "own_pivots",
        shape((count, rank), jnp.bfloat16),
        first_point.reshape(1),
        packed,
        pivot_row,
        scalars=1,
        flops=2 * count * row_count * rank,
    )
    pivot_here = (pivot_row // row_count % width == lax.axis_index("x")).astype(jnp.int32)

    def fetch(shift):
        def branch(data, part):
            spread = jnp.broadcast_to(part[None], (size_of(SECOND_SUM),) + part.shape)
            some = jnp.sum(exchanged(spread, SECOND_SUM), axis=0)
            pieces = lax.optimization_barrier(from_partner(data, shift))
            return pieces, some

        return branch

    pieces, pivot_some = lax.switch(
        round_index[0] - 1, [fetch(k) for k in range(1, MAX_SHIFT + 1)], quad, pivot_part
    )
    spread = jnp.broadcast_to(pivot_some[None], (size_of(FIRST_SUM), count, rank))
    pivot_all = exchanged(spread, FIRST_SUM)

    product_scale = 8.0 / math.sqrt(block_points)
    flops = (width * row_count) ** 2 * (count + EXTRA + probe_count)
    exps = (width * row_count) ** 2 // 2
    ahead = ((lax.axis_index("x") + lax.axis_index(GROUP_AXES) + 1) % 2).astype(jnp.int32).reshape(1)
    first, quadratic_part, row_all, col_all = local(
        functools.partial(
            first_half_kernel,
            count=count,
            scale=2.0 * product_scale / math.sqrt(total_points),
        ),
        "first_half",
        (
            shape((width, probe_count, row_count), jnp.float32),
            shape((probe_count, rank), jnp.float32),
            shape((width, count + EXTRA, row_count), jnp.bfloat16),
            shape((width, row_count, count + EXTRA), jnp.bfloat16),
        ),
        ahead,
        quad,
        pieces,
        scalars=1,
        flops=flops,
        exps=exps,
    )
    packed_sums = (probe_count + 1) * rank
    spread = local(
        functools.partial(projection_kernel, count=count),
        "projection",
        shape((size_of(FIRST_SUM), 1, packed_sums), jnp.float32),
        pivot_all,
        pivot_here,
        quad,
        quadratic_part,
        flops=2 * width * row_count * rank * (count + EXTRA + probe_count),
        exps=width * row_count * rank,
    )
    some = exchanged(spread, FIRST_SUM)
    sums = local(
        functools.partial(second_half_kernel, count=count, scale=product_scale),
        "second_half",
        shape((width, probe_count, row_count), jnp.float32),
        ahead,
        row_all,
        col_all,
        pieces,
        first,
        scalars=1,
        flops=flops,
        exps=exps,
    )
    spread = local(
        sum_spread_kernel,
        "first_sum",
        shape((size_of(SECOND_SUM), 1, packed_sums), jnp.float32),
        some,
    )
    parts = local(
        join_kernel,
        "join",
        shape((width, probe_count, row_count + 2 * rank), jnp.float32),
        sums,
        exchanged(spread, SECOND_SUM),
    )
    product, projection, quadratic = local(
        functools.partial(finish_kernel, projection_scale=8.0 / math.sqrt(total_points)),
        "finish",
        (
            shape((probe_count, row_count), jnp.float32),
            shape((probe_count, rank), jnp.float32),
            shape((probe_count,), jnp.float32),
        ),
        exchanged(parts, "x"),
    )
    return product, projection, quadratic


def solution(mesh):
    fine = Mesh(mesh.devices.reshape(Y, ZLO, CORE, ZHI, X), ALL_AXES)
    split = P(None, ALL_AXES)
    return jax.shard_map(
        body,
        mesh=fine,
        in_specs=(split, split, P(), P(), P()),
        out_specs=(split, P(), P()),
        check_vma=False,
    )
```

```python
import functools
import math

import jax
import jax.numpy as jnp
from jax import lax
from jax.experimental import pallas as pl
from jax.experimental.pallas import tpu as pltpu
from jax.sharding import Mesh
from jax.sharding import PartitionSpec as P

Y, ZLO, CORE, ZHI, X = 8, 4, 2, 2, 4
GROUP_AXES = ("y", "zlo", "core")
ALL_AXES = ("y", "zlo", "core", "zhi", "x")
FIRST_SUM, SECOND_SUM = ("y", "core"), ("zlo", "zhi")
MAX_SHIFT = 31
EXTRA = 16
VMEM_LIMIT = 48 * 2**20


def size_of(axes):
    return lax.axis_size(axes)


def exchanged(x, axes):
    return lax.all_to_all(x, axes, 0, 0)


def from_partner(x, shift):
    groups, halves, width = size_of(GROUP_AXES), size_of("zhi"), size_of("x")
    pairs = []
    for group in range(groups):
        for half in range(halves):
            for place in range(width):
                way = 1 - 2 * ((place + group) % 2)
                source = (group + way * shift) % groups
                source = (source * halves + (half ^ place // 2)) * width + place
                pairs.append((source, (group * halves + half) * width + place))
    return lax.ppermute(x, ALL_AXES, pairs)


def local(
    kernel, name, out_shape, *args, scalars=0, flops=0, exps=0, scratch=(), space=pltpu.VMEM, room=VMEM_LIMIT
):
    moved = sum(math.prod(a.shape) * a.dtype.itemsize for a in args)
    specs = [pl.BlockSpec(memory_space=pltpu.SMEM)] * scalars
    specs += [pl.BlockSpec(memory_space=space)] * (len(args) - scalars)
    return pl.pallas_call(
        kernel,
        name=name,
        out_shape=out_shape,
        in_specs=specs,
        out_specs=jax.tree.map(lambda _: pl.BlockSpec(memory_space=pltpu.VMEM), out_shape),
        scratch_shapes=scratch,
        cost_estimate=pl.CostEstimate(flops=flops, bytes_accessed=moved, transcendentals=exps),
        compiler_params=pltpu.CompilerParams(vmem_limit_bytes=room),
    )(*args)


def extended(feat, ones_first):
    wide = feat.astype(jnp.float32)
    half = -0.5 * jnp.sum(wide * wide, axis=0, keepdims=True)
    high = half.astype(jnp.bfloat16).astype(jnp.float32)
    middle = (half - high).astype(jnp.bfloat16).astype(jnp.float32)
    low = half - high - middle
    row = lax.broadcasted_iota(jnp.int32, (EXTRA, feat.shape[1]), 0)
    ones, norm = (0, 3) if ones_first else (3, 0)
    rest = jnp.where((row >= ones) & (row < ones + 3), 1.0, 0.0)
    for offset, piece in enumerate((high, middle, low)):
        rest = jnp.where(row == norm + offset, piece, rest)
    return jnp.concatenate([feat, rest.astype(jnp.bfloat16)], axis=0)


def turned(x):
    return x.astype(jnp.float32).T.astype(jnp.bfloat16)


def prepare_kernel(feat_hbm, scale_hbm, probe_hbm, out_ref, feat_ref, scale_ref, probe_ref, done):
    copies = [
        pltpu.make_async_copy(source, target, done.at[index])
        for index, (source, target) in enumerate(
            ((feat_hbm, feat_ref), (scale_hbm, scale_ref), (probe_hbm, probe_ref))
        )
    ]
    for copy in copies:
        copy.start()
    for copy in copies:
        copy.wait()
    count = feat_ref.shape[0]
    row = lax.broadcasted_iota(jnp.int32, (count, count), 0)
    col = lax.broadcasted_iota(jnp.int32, (count, count), 1)
    spread = jnp.broadcast_to(scale_ref[...], (count, count))
    scale = jnp.sum(jnp.where(row == col, spread, 0.0), axis=1, keepdims=True)
    scaled = (feat_ref[...] * jnp.sqrt(scale)).astype(jnp.bfloat16)
    packed = jnp.concatenate([scaled, probe_ref[...]], axis=0)
    for copy in range(out_ref.shape[0]):
        out_ref[copy] = packed


def own_pivots_kernel(first_ref, packed_ref, pivot_ref, out_ref):
    count, rank = out_ref.shape
    points = packed_ref.shape[2]
    point = lax.broadcasted_iota(jnp.int32, (points, rank), 0) + first_ref[0]
    mask = jnp.where(point == pivot_ref[...], 1.0, 0.0).astype(jnp.bfloat16)
    part = jnp.dot(packed_ref[0, :count], mask, preferred_element_type=jnp.float32)
    out_ref[...] = part.astype(jnp.bfloat16)


def sum_spread_kernel(in_ref, out_ref):
    total = in_ref[0].astype(jnp.float32)
    for peer in range(1, in_ref.shape[0]):
        total = total + in_ref[peer].astype(jnp.float32)
    for copy in range(out_ref.shape[0]):
        out_ref[copy] = total.astype(out_ref.dtype)


def pair_sum(row_all, col_all, col_ref, place, other, count, probes):
    power = jnp.dot(col_all[other], row_all[place], preferred_element_type=jnp.float32)
    kernel = jnp.exp(power).astype(jnp.bfloat16)
    col_probe = col_ref[other, count : count + probes]
    return jnp.dot(col_probe, kernel, preferred_element_type=jnp.float32)


def first_half_kernel(
    ahead_ref,
    row_ref,
    col_ref,
    pivot_ref,
    here_ref,
    sum_ref,
    out_ref,
    row_all,
    col_all,
    *,
    count,
    scale,
):
    width, probes = row_ref.shape[0], sum_ref.shape[1]
    ahead = ahead_ref[0] == 1
    for place in range(width):
        row_all[place] = extended(row_ref[place, :count], True)
        col_all[place] = turned(extended(col_ref[place, :count], False))
    sum_ref[...] = jnp.zeros_like(sum_ref)

    def step(turn, carry):
        for part in range(4):
            place = jnp.where(ahead, 2 * turn + part // 2, 2 + turn)
            other = jnp.where(ahead, part % 2, part)
            sum_ref[place] += pair_sum(row_all, col_all, col_ref, place, other, count, probes)
        return carry

    lax.fori_loop(0, 2, step, 0)
    quad = jnp.zeros((probes, 1), jnp.float32)
    for place in range(width):
        row_probe = row_ref[place, count : count + probes].astype(jnp.float32)
        quad = quad + jnp.sum(row_probe * sum_ref[place], axis=1, keepdims=True)
    rank = pivot_ref.shape[2]
    pivot = pivot_ref[0].astype(jnp.float32)
    for peer in range(1, pivot_ref.shape[0]):
        pivot = pivot + pivot_ref[peer].astype(jnp.float32)
    pivot = turned(extended(pivot.astype(jnp.bfloat16), False))
    total = jnp.zeros((probes, rank), jnp.float32)
    for place in range(width):
        power = jnp.dot(pivot, row_all[place], preferred_element_type=jnp.float32)
        kernel = jnp.exp(power).astype(jnp.bfloat16)
        total = total + lax.dot_general(
            row_ref[place, count : count + probes],
            kernel,
            (((1,), (1,)), ((), ())),
            preferred_element_type=jnp.float32,
        )
    total = jnp.where(here_ref[...] != 0, total, 0.0)
    rows = [total[probe : probe + 1] for probe in range(probes)]
    row = lax.broadcasted_iota(jnp.int32, (probes, rank), 0)
    lane = lax.broadcasted_iota(jnp.int32, (probes, rank), 1)
    quad = jnp.broadcast_to(scale * quad, (probes, rank))
    rows.append(jnp.sum(jnp.where(row == lane, quad, 0.0), axis=0, keepdims=True))
    packed = jnp.concatenate(rows, axis=1)
    for copy in range(out_ref.shape[0]):
        out_ref[copy] = packed


def second_half_kernel(
    ahead_ref, row_all, col_all, col_ref, first_ref, sum_ref, *, count, scale
):
    width, probes = first_ref.shape[:2]
    ahead = ahead_ref[0] == 1
    sum_ref[...] = first_ref[...]

    def step(turn, carry):
        for part in range(4):
            place = jnp.where(ahead, 2 * turn + part // 2, turn)
            other = jnp.where(ahead, 2 + part % 2, part)
            sum_ref[place] += pair_sum(row_all, col_all, col_ref, place, other, count, probes)
        return carry

    lax.fori_loop(0, 2, step, 0)
    for place in range(width):
        sum_ref[place] = scale * sum_ref[place]


def join_kernel(sum_ref, total_ref, out_ref):
    width, probes, points = sum_ref.shape
    rank = (out_ref.shape[2] - points) // 2
    total = total_ref[0]
    for peer in range(1, total_ref.shape[0]):
        total = total + total_ref[peer]
    rows = [total[:, probe * rank : (probe + 1) * rank] for probe in range(probes)]
    last = jnp.broadcast_to(total[:, probes * rank :], (probes, rank))
    joined = jnp.concatenate([jnp.concatenate(rows, axis=0), last], axis=1)
    for place in range(width):
        out_ref[place, :, :points] = sum_ref[place]
        out_ref[place, :, points:] = joined


def finish_kernel(in_ref, product_ref, projection_ref, quadratic_ref, *, projection_scale):
    probes, points = product_ref.shape
    rank = projection_ref.shape[1]
    total = in_ref[0]
    for peer in range(1, in_ref.shape[0]):
        total = total + in_ref[peer]
    product_ref[...] = total[:, :points]
    projection_ref[...] = projection_scale * total[:, points : points + rank]
    quadratic_ref[...] = total[0, points + rank : points + rank + probes]


def body(features, probes, inverse_scales, round_index, pivots):
    count, row_count = features.shape
    probe_count, rank = probes.shape[0], pivots.shape[0]
    rows = count + probe_count
    width = size_of("x")
    block_points = row_count * size_of(("zhi", "x"))
    total_points = block_points * size_of(GROUP_AXES)
    shape = jax.ShapeDtypeStruct

    packed = local(
        prepare_kernel,
        "prepare",
        shape((width, rows, row_count), jnp.bfloat16),
        features,
        inverse_scales.reshape(1, count),
        probes,
        scratch=(
            pltpu.VMEM(features.shape, features.dtype),
            pltpu.VMEM((1, count), inverse_scales.dtype),
            pltpu.VMEM(probes.shape, probes.dtype),
            pltpu.SemaphoreType.DMA((3,)),
        ),
        space=pltpu.HBM,
        room=60 * 2**20,
    )
    quad = exchanged(packed, "x")

    first_point = (lax.axis_index(ALL_AXES) * row_count).astype(jnp.int32)
    pivot_row = pivots.reshape(1, rank)
    pivot_part = local(
        own_pivots_kernel,
        "own_pivots",
        shape((count, rank), jnp.bfloat16),
        first_point.reshape(1),
        packed,
        pivot_row,
        scalars=1,
        flops=2 * count * row_count * rank,
    )
    pivot_here = (pivot_row // row_count % width == lax.axis_index("x")).astype(jnp.int32)

    def fetch(shift):
        def branch(data, part):
            spread = jnp.broadcast_to(part[None], (size_of(SECOND_SUM),) + part.shape)
            some = local(
                sum_spread_kernel,
                "pivot_sum",
                shape((size_of(FIRST_SUM), count, rank), jnp.bfloat16),
                exchanged(spread, SECOND_SUM),
            )
            pieces = from_partner(data, shift)
            return pieces, exchanged(some, FIRST_SUM)

        return branch

    pieces, pivot_all = lax.switch(
        round_index[0] - 1, [fetch(k) for k in range(1, MAX_SHIFT + 1)], quad, pivot_part
    )

    product_scale = 8.0 / math.sqrt(block_points)
    flops = (width * row_count) ** 2 * (count + EXTRA + probe_count)
    exps = (width * row_count) ** 2 // 2
    ahead = ((lax.axis_index("x") + lax.axis_index(GROUP_AXES) + 1) % 2).astype(jnp.int32).reshape(1)
    packed_sums = (probe_count + 1) * rank
    first, spread, row_all, col_all = local(
        functools.partial(
            first_half_kernel,
            count=count,
            scale=2.0 * product_scale / math.sqrt(total_points),
        ),
        "first_half",
        (
            shape((width, probe_count, row_count), jnp.float32),
            shape((size_of(FIRST_SUM), 1, packed_sums), jnp.float32),
            shape((width, count + EXTRA, row_count), jnp.bfloat16),
            shape((width, row_count, count + EXTRA), jnp.bfloat16),
        ),
        ahead,
        quad,
        pieces,
        pivot_all,
        pivot_here,
        scalars=1,
        flops=flops,
        exps=exps,
    )
    some = exchanged(spread, FIRST_SUM)
    sums = local(
        functools.partial(second_half_kernel, count=count, scale=product_scale),
        "second_half",
        shape((width, probe_count, row_count), jnp.float32),
        ahead,
        row_all,
        col_all,
        pieces,
        first,
        scalars=1,
        flops=flops,
        exps=exps,
    )
    spread = local(
        sum_spread_kernel,
        "first_sum",
        shape((size_of(SECOND_SUM), 1, packed_sums), jnp.float32),
        some,
    )
    parts = local(
        join_kernel,
        "join",
        shape((width, probe_count, row_count + 2 * rank), jnp.float32),
        sums,
        exchanged(spread, SECOND_SUM),
    )
    product, projection, quadratic = local(
        functools.partial(finish_kernel, projection_scale=8.0 / math.sqrt(total_points)),
        "finish",
        (
            shape((probe_count, row_count), jnp.float32),
            shape((probe_count, rank), jnp.float32),
            shape((probe_count,), jnp.float32),
        ),
        exchanged(parts, "x"),
    )
    return product, projection, quadratic


def solution(mesh):
    fine = Mesh(mesh.devices.reshape(Y, ZLO, CORE, ZHI, X), ALL_AXES)
    split = P(None, ALL_AXES)
    return jax.shard_map(
        body,
        mesh=fine,
        in_specs=(split, split, P(), P(), P()),
        out_specs=(split, P(), P()),
        check_vma=False,
    )
```

```python
import functools
import math

import jax
import jax.numpy as jnp
from jax import lax
from jax.experimental import pallas as pl
from jax.experimental.pallas import tpu as pltpu
from jax.sharding import Mesh
from jax.sharding import PartitionSpec as P

Y, ZLO, CORE, ZHI, X = 8, 4, 2, 2, 4
GROUP_AXES = ("y", "zlo", "core")
ALL_AXES = ("y", "zlo", "core", "zhi", "x")
FIRST_SUM, SECOND_SUM = ("y", "core"), ("zlo", "zhi")
MAX_SHIFT = 31
EXTRA = 16
VMEM_LIMIT = 48 * 2**20


def size_of(axes):
    return lax.axis_size(axes)


def exchanged(x, axes):
    return lax.all_to_all(x, axes, 0, 0)


def from_partner(x, shift):
    groups, halves, width = size_of(GROUP_AXES), size_of("zhi"), size_of("x")
    pairs = []
    for group in range(groups):
        for half in range(halves):
            for place in range(width):
                way = 1 - 2 * ((place + group) % 2)
                source = (group + way * shift) % groups
                source = (source * halves + (half ^ place // 2)) * width + place
                pairs.append((source, (group * halves + half) * width + place))
    return lax.ppermute(x, ALL_AXES, pairs)


def local(
    kernel, name, out_shape, *args, scalars=0, flops=0, exps=0, scratch=(), space=pltpu.VMEM, room=VMEM_LIMIT
):
    moved = sum(math.prod(a.shape) * a.dtype.itemsize for a in args)
    specs = [pl.BlockSpec(memory_space=pltpu.SMEM)] * scalars
    specs += [pl.BlockSpec(memory_space=space)] * (len(args) - scalars)
    return pl.pallas_call(
        kernel,
        name=name,
        out_shape=out_shape,
        in_specs=specs,
        out_specs=jax.tree.map(lambda _: pl.BlockSpec(memory_space=pltpu.VMEM), out_shape),
        scratch_shapes=scratch,
        cost_estimate=pl.CostEstimate(flops=flops, bytes_accessed=moved, transcendentals=exps),
        compiler_params=pltpu.CompilerParams(vmem_limit_bytes=room),
    )(*args)


def extended(feat, ones_first):
    wide = feat.astype(jnp.float32)
    half = -0.5 * jnp.sum(wide * wide, axis=0, keepdims=True)
    high = half.astype(jnp.bfloat16).astype(jnp.float32)
    middle = (half - high).astype(jnp.bfloat16).astype(jnp.float32)
    low = half - high - middle
    row = lax.broadcasted_iota(jnp.int32, (EXTRA, feat.shape[1]), 0)
    ones, norm = (0, 3) if ones_first else (3, 0)
    rest = jnp.where((row >= ones) & (row < ones + 3), 1.0, 0.0)
    for offset, piece in enumerate((high, middle, low)):
        rest = jnp.where(row == norm + offset, piece, rest)
    return jnp.concatenate([feat, rest.astype(jnp.bfloat16)], axis=0)


def turned(x):
    return x.astype(jnp.float32).T.astype(jnp.bfloat16)


def prepare_kernel(feat_hbm, scale_hbm, probe_hbm, out_ref, feat_ref, scale_ref, probe_ref, done):
    copies = [
        pltpu.make_async_copy(source, target, done.at[index])
        for index, (source, target) in enumerate(
            ((feat_hbm, feat_ref), (scale_hbm, scale_ref), (probe_hbm, probe_ref))
        )
    ]
    for copy in copies:
        copy.start()
    for copy in copies:
        copy.wait()
    count = feat_ref.shape[0]
    row = lax.broadcasted_iota(jnp.int32, (count, count), 0)
    col = lax.broadcasted_iota(jnp.int32, (count, count), 1)
    spread = jnp.broadcast_to(scale_ref[...], (count, count))
    scale = jnp.sum(jnp.where(row == col, spread, 0.0), axis=1, keepdims=True)
    scaled = (feat_ref[...] * jnp.sqrt(scale)).astype(jnp.bfloat16)
    packed = jnp.concatenate([scaled, probe_ref[...]], axis=0)
    for copy in range(out_ref.shape[0]):
        out_ref[copy] = packed


def own_pivots_kernel(first_ref, packed_ref, pivot_ref, out_ref):
    count, rank = out_ref.shape[1:]
    points = packed_ref.shape[2]
    point = lax.broadcasted_iota(jnp.int32, (points, rank), 0) + first_ref[0]
    mask = jnp.where(point == pivot_ref[...], 1.0, 0.0).astype(jnp.bfloat16)
    part = jnp.dot(packed_ref[0, :count], mask, preferred_element_type=jnp.float32)
    for copy in range(out_ref.shape[0]):
        out_ref[copy] = part.astype(jnp.bfloat16)


def sum_spread_kernel(in_ref, out_ref):
    total = in_ref[0].astype(jnp.float32)
    for peer in range(1, in_ref.shape[0]):
        total = total + in_ref[peer].astype(jnp.float32)
    for copy in range(out_ref.shape[0]):
        out_ref[copy] = total.astype(out_ref.dtype)


def pair_sum(row_all, col_all, col_ref, place, other, count, probes):
    power = jnp.dot(col_all[other], row_all[place], preferred_element_type=jnp.float32)
    kernel = jnp.exp(power).astype(jnp.bfloat16)
    col_probe = col_ref[other, count : count + probes]
    return jnp.dot(col_probe, kernel, preferred_element_type=jnp.float32)


def first_half_kernel(
    ahead_ref,
    row_ref,
    col_ref,
    pivot_ref,
    here_ref,
    sum_ref,
    out_ref,
    row_all,
    col_all,
    *,
    count,
    scale,
):
    width, probes = row_ref.shape[0], sum_ref.shape[1]
    ahead = ahead_ref[0] == 1
    for place in range(width):
        row_all[place] = extended(row_ref[place, :count], True)
        col_all[place] = turned(extended(col_ref[place, :count], False))
    sum_ref[...] = jnp.zeros_like(sum_ref)

    def step(turn, carry):
        for part in range(4):
            place = jnp.where(ahead, 2 * turn + part // 2, 2 + turn)
            other = jnp.where(ahead, part % 2, part)
            sum_ref[place] += pair_sum(row_all, col_all, col_ref, place, other, count, probes)
        return carry

    lax.fori_loop(0, 2, step, 0)
    quad = jnp.zeros((probes, 1), jnp.float32)
    for place in range(width):
        row_probe = row_ref[place, count : count + probes].astype(jnp.float32)
        quad = quad + jnp.sum(row_probe * sum_ref[place], axis=1, keepdims=True)
    rank = pivot_ref.shape[2]
    pivot = pivot_ref[0].astype(jnp.float32)
    for peer in range(1, pivot_ref.shape[0]):
        pivot = pivot + pivot_ref[peer].astype(jnp.float32)
    pivot = turned(extended(pivot.astype(jnp.bfloat16), False))
    total = jnp.zeros((probes, rank), jnp.float32)
    for place in range(width):
        power = jnp.dot(pivot, row_all[place], preferred_element_type=jnp.float32)
        kernel = jnp.exp(power).astype(jnp.bfloat16)
        total = total + lax.dot_general(
            row_ref[place, count : count + probes],
            kernel,
            (((1,), (1,)), ((), ())),
            preferred_element_type=jnp.float32,
        )
    total = jnp.where(here_ref[...] != 0, total, 0.0)
    rows = [total[probe : probe + 1] for probe in range(probes)]
    row = lax.broadcasted_iota(jnp.int32, (probes, rank), 0)
    lane = lax.broadcasted_iota(jnp.int32, (probes, rank), 1)
    quad = jnp.broadcast_to(scale * quad, (probes, rank))
    rows.append(jnp.sum(jnp.where(row == lane, quad, 0.0), axis=0, keepdims=True))
    packed = jnp.concatenate(rows, axis=1)
    for copy in range(out_ref.shape[0]):
        out_ref[copy] = packed


def second_half_kernel(
    ahead_ref, row_all, col_all, col_ref, first_ref, sum_ref, *, count, scale
):
    width, probes = first_ref.shape[:2]
    ahead = ahead_ref[0] == 1
    sum_ref[...] = first_ref[...]

    def step(turn, carry):
        for part in range(4):
            place = jnp.where(ahead, 2 * turn + part // 2, turn)
            other = jnp.where(ahead, 2 + part % 2, part)
            sum_ref[place] += pair_sum(row_all, col_all, col_ref, place, other, count, probes)
        return carry

    lax.fori_loop(0, 2, step, 0)
    for place in range(width):
        sum_ref[place] = scale * sum_ref[place]


def join_kernel(sum_ref, total_ref, out_ref):
    width, probes, points = sum_ref.shape
    rank = (out_ref.shape[2] - points) // 2
    total = total_ref[0]
    for peer in range(1, total_ref.shape[0]):
        total = total + total_ref[peer]
    rows = [total[:, probe * rank : (probe + 1) * rank] for probe in range(probes)]
    last = jnp.broadcast_to(total[:, probes * rank :], (probes, rank))
    joined = jnp.concatenate([jnp.concatenate(rows, axis=0), last], axis=1)
    for place in range(width):
        out_ref[place, :, :points] = sum_ref[place]
        out_ref[place, :, points:] = joined


def finish_kernel(in_ref, product_ref, projection_ref, quadratic_ref, *, projection_scale):
    probes, points = product_ref.shape
    rank = projection_ref.shape[1]
    total = in_ref[0]
    for peer in range(1, in_ref.shape[0]):
        total = total + in_ref[peer]
    product_ref[...] = total[:, :points]
    projection_ref[...] = projection_scale * total[:, points : points + rank]
    quadratic_ref[...] = total[0, points + rank : points + rank + probes]


def body(features, probes, inverse_scales, round_index, pivots):
    count, row_count = features.shape
    probe_count, rank = probes.shape[0], pivots.shape[0]
    rows = count + probe_count
    width = size_of("x")
    block_points = row_count * size_of(("zhi", "x"))
    total_points = block_points * size_of(GROUP_AXES)
    shape = jax.ShapeDtypeStruct

    packed = local(
        prepare_kernel,
        "prepare",
        shape((width, rows, row_count), jnp.bfloat16),
        features,
        inverse_scales.reshape(1, count),
        probes,
        scratch=(
            pltpu.VMEM(features.shape, features.dtype),
            pltpu.VMEM((1, count), inverse_scales.dtype),
            pltpu.VMEM(probes.shape, probes.dtype),
            pltpu.SemaphoreType.DMA((3,)),
        ),
        space=pltpu.HBM,
        room=60 * 2**20,
    )
    quad = exchanged(packed, "x")

    first_point = (lax.axis_index(ALL_AXES) * row_count).astype(jnp.int32)
    pivot_row = pivots.reshape(1, rank)
    pivot_part = local(
        own_pivots_kernel,
        "own_pivots",
        shape((size_of(SECOND_SUM), count, rank), jnp.bfloat16),
        first_point.reshape(1),
        packed,
        pivot_row,
        scalars=1,
        flops=2 * count * row_count * rank,
    )
    pivot_here = (pivot_row // row_count % width == lax.axis_index("x")).astype(jnp.int32)

    def fetch(shift):
        def branch(data, part):
            some = local(
                sum_spread_kernel,
                "pivot_sum",
                shape((size_of(FIRST_SUM), count, rank), jnp.bfloat16),
                exchanged(part, SECOND_SUM),
            )
            pieces = from_partner(data, shift)
            return pieces, exchanged(some, FIRST_SUM)

        return branch

    pieces, pivot_all = lax.switch(
        round_index[0] - 1, [fetch(k) for k in range(1, MAX_SHIFT + 1)], quad, pivot_part
    )

    product_scale = 8.0 / math.sqrt(block_points)
    flops = (width * row_count) ** 2 * (count + EXTRA + probe_count)
    exps = (width * row_count) ** 2 // 2
    ahead = ((lax.axis_index("x") + lax.axis_index(GROUP_AXES) + 1) % 2).astype(jnp.int32).reshape(1)
    packed_sums = (probe_count + 1) * rank
    first, spread, row_all, col_all = local(
        functools.partial(
            first_half_kernel,
            count=count,
            scale=2.0 * product_scale / math.sqrt(total_points),
        ),
        "first_half",
        (
            shape((width, probe_count, row_count), jnp.float32),
            shape((size_of(FIRST_SUM), 1, packed_sums), jnp.float32),
            shape((width, count + EXTRA, row_count), jnp.bfloat16),
            shape((width, row_count, count + EXTRA), jnp.bfloat16),
        ),
        ahead,
        quad,
        pieces,
        pivot_all,
        pivot_here,
        scalars=1,
        flops=flops,
        exps=exps,
    )
    some = exchanged(spread, FIRST_SUM)
    sums = local(
        functools.partial(second_half_kernel, count=count, scale=product_scale),
        "second_half",
        shape((width, probe_count, row_count), jnp.float32),
        ahead,
        row_all,
        col_all,
        pieces,
        first,
        scalars=1,
        flops=flops,
        exps=exps,
    )
    spread = local(
        sum_spread_kernel,
        "first_sum",
        shape((size_of(SECOND_SUM), 1, packed_sums), jnp.float32),
        some,
    )
    parts = local(
        join_kernel,
        "join",
        shape((width, probe_count, row_count + 2 * rank), jnp.float32),
        sums,
        exchanged(spread, SECOND_SUM),
    )
    product, projection, quadratic = local(
        functools.partial(finish_kernel, projection_scale=8.0 / math.sqrt(total_points)),
        "finish",
        (
            shape((probe_count, row_count), jnp.float32),
            shape((probe_count, rank), jnp.float32),
            shape((probe_count,), jnp.float32),
        ),
        exchanged(parts, "x"),
    )
    return product, projection, quadratic


def solution(mesh):
    fine = Mesh(mesh.devices.reshape(Y, ZLO, CORE, ZHI, X), ALL_AXES)
    split = P(None, ALL_AXES)
    return jax.shard_map(
        body,
        mesh=fine,
        in_specs=(split, split, P(), P(), P()),
        out_specs=(split, P(), P()),
        check_vma=False,
    )
```

```python
import functools
import math

import jax
import jax.numpy as jnp
from jax import lax
from jax.experimental import pallas as pl
from jax.experimental.pallas import tpu as pltpu
from jax.sharding import Mesh
from jax.sharding import PartitionSpec as P

Y, ZLO, CORE, ZHI, X = 8, 4, 2, 2, 4
GROUP_AXES = ("y", "zlo", "core")
ALL_AXES = ("y", "zlo", "core", "zhi", "x")
FIRST_SUM, SECOND_SUM = ("y", "core"), ("zlo", "zhi")
MAX_SHIFT = 31
EXTRA = 16
VMEM_LIMIT = 48 * 2**20


def size_of(axes):
    return lax.axis_size(axes)


def exchanged(x, axes):
    return lax.all_to_all(x, axes, 0, 0)


def from_partner(x, shift):
    groups, halves, width = size_of(GROUP_AXES), size_of("zhi"), size_of("x")
    pairs = []
    for group in range(groups):
        for half in range(halves):
            for place in range(width):
                way = 1 - 2 * ((place + group) % 2)
                source = (group + way * shift) % groups
                source = (source * halves + (half ^ place // 2)) * width + place
                pairs.append((source, (group * halves + half) * width + place))
    return lax.ppermute(x, ALL_AXES, pairs)


def local(
    kernel, name, out_shape, *args, scalars=0, flops=0, exps=0, scratch=(), space=pltpu.VMEM, room=VMEM_LIMIT
):
    moved = sum(math.prod(a.shape) * a.dtype.itemsize for a in args)
    specs = [pl.BlockSpec(memory_space=pltpu.SMEM)] * scalars
    specs += [pl.BlockSpec(memory_space=space)] * (len(args) - scalars)
    return pl.pallas_call(
        kernel,
        name=name,
        out_shape=out_shape,
        in_specs=specs,
        out_specs=jax.tree.map(lambda _: pl.BlockSpec(memory_space=pltpu.VMEM), out_shape),
        scratch_shapes=scratch,
        cost_estimate=pl.CostEstimate(flops=flops, bytes_accessed=moved, transcendentals=exps),
        compiler_params=pltpu.CompilerParams(vmem_limit_bytes=room),
    )(*args)


def extended(feat, ones_first):
    wide = feat.astype(jnp.float32)
    half = -0.5 * jnp.sum(wide * wide, axis=0, keepdims=True)
    high = half.astype(jnp.bfloat16).astype(jnp.float32)
    middle = (half - high).astype(jnp.bfloat16).astype(jnp.float32)
    low = half - high - middle
    row = lax.broadcasted_iota(jnp.int32, (EXTRA, feat.shape[1]), 0)
    ones, norm = (0, 3) if ones_first else (3, 0)
    rest = jnp.where((row >= ones) & (row < ones + 3), 1.0, 0.0)
    for offset, piece in enumerate((high, middle, low)):
        rest = jnp.where(row == norm + offset, piece, rest)
    return jnp.concatenate([feat, rest.astype(jnp.bfloat16)], axis=0)


def turned(x):
    return x.astype(jnp.float32).T.astype(jnp.bfloat16)


def prepare_kernel(feat_hbm, scale_hbm, probe_hbm, out_ref, feat_ref, scale_ref, probe_ref, done):
    copies = [
        pltpu.make_async_copy(source, target, done.at[index])
        for index, (source, target) in enumerate(
            ((feat_hbm, feat_ref), (scale_hbm, scale_ref), (probe_hbm, probe_ref))
        )
    ]
    for copy in copies:
        copy.start()
    for copy in copies:
        copy.wait()
    count = feat_ref.shape[0]
    row = lax.broadcasted_iota(jnp.int32, (count, count), 0)
    col = lax.broadcasted_iota(jnp.int32, (count, count), 1)
    spread = jnp.broadcast_to(scale_ref[...], (count, count))
    scale = jnp.sum(jnp.where(row == col, spread, 0.0), axis=1, keepdims=True)
    scaled = (feat_ref[...] * jnp.sqrt(scale)).astype(jnp.bfloat16)
    packed = jnp.concatenate([scaled, probe_ref[...]], axis=0)
    for copy in range(out_ref.shape[0]):
        out_ref[copy] = packed


def own_pivots_kernel(first_ref, packed_ref, pivot_ref, out_ref):
    count, rank = out_ref.shape[1:]
    points = packed_ref.shape[2]
    point = lax.broadcasted_iota(jnp.int32, (points, rank), 0) + first_ref[0]
    mask = jnp.where(point == pivot_ref[...], 1.0, 0.0).astype(jnp.bfloat16)
    part = jnp.dot(packed_ref[0, :count], mask, preferred_element_type=jnp.float32)
    for copy in range(out_ref.shape[0]):
        out_ref[copy] = part.astype(jnp.bfloat16)


def sum_spread_kernel(in_ref, out_ref):
    total = in_ref[0].astype(jnp.float32)
    for peer in range(1, in_ref.shape[0]):
        total = total + in_ref[peer].astype(jnp.float32)
    for copy in range(out_ref.shape[0]):
        out_ref[copy] = total.astype(out_ref.dtype)


def pair_sum(row_all, col_all, col_probe, place, other):
    power = jnp.dot(col_all[other], row_all[place], preferred_element_type=jnp.float32)
    kernel = jnp.exp(power).astype(jnp.bfloat16)
    return jnp.dot(col_probe[other], kernel, preferred_element_type=jnp.float32)


def first_half_kernel(
    ahead_ref,
    row_ref,
    col_ref,
    pivot_ref,
    here_ref,
    sum_ref,
    out_ref,
    row_all,
    col_all,
    col_probe,
    *,
    count,
    scale,
):
    width, probes = row_ref.shape[0], sum_ref.shape[1]
    ahead = ahead_ref[0] == 1
    for place in range(width):
        row_all[place] = extended(row_ref[place, :count], True)
        col_all[place] = turned(extended(col_ref[place, :count], False))
        col_probe[place] = col_ref[place, count : count + probes]
    sum_ref[...] = jnp.zeros_like(sum_ref)

    def step(turn, carry):
        for part in range(2):
            place = jnp.where(ahead, 2 * turn + part, 2 + turn)
            first = jnp.where(ahead, 0, 2 * part)
            sum_ref[place] += pair_sum(row_all, col_all, col_probe, place, first) + pair_sum(
                row_all, col_all, col_probe, place, first + 1
            )
        return carry

    for turn in range(2):
        step(turn, 0)
    quad = jnp.zeros((probes, 1), jnp.float32)
    for place in range(width):
        row_probe = row_ref[place, count : count + probes].astype(jnp.float32)
        quad = quad + jnp.sum(row_probe * sum_ref[place], axis=1, keepdims=True)
    rank = pivot_ref.shape[2]
    pivot = pivot_ref[0].astype(jnp.float32)
    for peer in range(1, pivot_ref.shape[0]):
        pivot = pivot + pivot_ref[peer].astype(jnp.float32)
    pivot = turned(extended(pivot.astype(jnp.bfloat16), False))
    total = jnp.zeros((probes, rank), jnp.float32)
    for place in range(width):
        power = jnp.dot(pivot, row_all[place], preferred_element_type=jnp.float32)
        kernel = jnp.exp(power).astype(jnp.bfloat16)
        total = total + lax.dot_general(
            row_ref[place, count : count + probes],
            kernel,
            (((1,), (1,)), ((), ())),
            preferred_element_type=jnp.float32,
        )
    total = jnp.where(here_ref[...] != 0, total, 0.0)
    rows = [total[probe : probe + 1] for probe in range(probes)]
    row = lax.broadcasted_iota(jnp.int32, (probes, rank), 0)
    lane = lax.broadcasted_iota(jnp.int32, (probes, rank), 1)
    quad = jnp.broadcast_to(scale * quad, (probes, rank))
    rows.append(jnp.sum(jnp.where(row == lane, quad, 0.0), axis=0, keepdims=True))
    packed = jnp.concatenate(rows, axis=1)
    for copy in range(out_ref.shape[0]):
        out_ref[copy] = packed


def second_half_kernel(ahead_ref, row_all, col_all, col_probe, first_ref, sum_ref, *, scale):
    width = first_ref.shape[0]
    ahead = ahead_ref[0] == 1
    sum_ref[...] = first_ref[...]

    def step(turn, carry):
        for part in range(4):
            place = jnp.where(ahead, 2 * turn + part // 2, turn)
            other = jnp.where(ahead, 2 + part % 2, part)
            sum_ref[place] += pair_sum(row_all, col_all, col_probe, place, other)
        return carry

    lax.fori_loop(0, 2, step, 0)
    for place in range(width):
        sum_ref[place] = scale * sum_ref[place]


def join_kernel(sum_ref, total_ref, out_ref):
    width, probes, points = sum_ref.shape
    rank = (out_ref.shape[2] - points) // 2
    total = total_ref[0]
    for peer in range(1, total_ref.shape[0]):
        total = total + total_ref[peer]
    rows = [total[:, probe * rank : (probe + 1) * rank] for probe in range(probes)]
    last = jnp.broadcast_to(total[:, probes * rank :], (probes, rank))
    joined = jnp.concatenate([jnp.concatenate(rows, axis=0), last], axis=1)
    for place in range(width):
        out_ref[place, :, :points] = sum_ref[place]
        out_ref[place, :, points:] = joined


def finish_kernel(in_ref, product_ref, projection_ref, quadratic_ref, *, projection_scale):
    probes, points = product_ref.shape
    rank = projection_ref.shape[1]
    total = in_ref[0]
    for peer in range(1, in_ref.shape[0]):
        total = total + in_ref[peer]
    product_ref[...] = total[:, :points]
    projection_ref[...] = projection_scale * total[:, points : points + rank]
    quadratic_ref[...] = total[0, points + rank : points + rank + probes]


def body(features, probes, inverse_scales, round_index, pivots):
    count, row_count = features.shape
    probe_count, rank = probes.shape[0], pivots.shape[0]
    rows = count + probe_count
    width = size_of("x")
    block_points = row_count * size_of(("zhi", "x"))
    total_points = block_points * size_of(GROUP_AXES)
    shape = jax.ShapeDtypeStruct

    packed = local(
        prepare_kernel,
        "prepare",
        shape((width, rows, row_count), jnp.bfloat16),
        features,
        inverse_scales.reshape(1, count),
        probes,
        scratch=(
            pltpu.VMEM(features.shape, features.dtype),
            pltpu.VMEM((1, count), inverse_scales.dtype),
            pltpu.VMEM(probes.shape, probes.dtype),
            pltpu.SemaphoreType.DMA((3,)),
        ),
        space=pltpu.HBM,
        room=60 * 2**20,
    )
    quad = exchanged(packed, "x")

    first_point = (lax.axis_index(ALL_AXES) * row_count).astype(jnp.int32)
    pivot_row = pivots.reshape(1, rank)
    pivot_part = local(
        own_pivots_kernel,
        "own_pivots",
        shape((size_of(SECOND_SUM), count, rank), jnp.bfloat16),
        first_point.reshape(1),
        packed,
        pivot_row,
        scalars=1,
        flops=2 * count * row_count * rank,
    )
    pivot_here = (pivot_row // row_count % width == lax.axis_index("x")).astype(jnp.int32)

    def fetch(shift):
        def branch(data, part):
            some = local(
                sum_spread_kernel,
                "pivot_sum",
                shape((size_of(FIRST_SUM), count, rank), jnp.bfloat16),
                exchanged(part, SECOND_SUM),
            )
            pieces = from_partner(data, shift)
            return pieces, exchanged(some, FIRST_SUM)

        return branch

    pieces, pivot_all = lax.switch(
        round_index[0] - 1, [fetch(k) for k in range(1, MAX_SHIFT + 1)], quad, pivot_part
    )

    product_scale = 8.0 / math.sqrt(block_points)
    flops = (width * row_count) ** 2 * (count + EXTRA + probe_count)
    exps = (width * row_count) ** 2 // 2
    ahead = ((lax.axis_index("x") + lax.axis_index(GROUP_AXES) + 1) % 2).astype(jnp.int32).reshape(1)
    packed_sums = (probe_count + 1) * rank
    first, spread, row_all, col_all, col_probe = local(
        functools.partial(
            first_half_kernel,
            count=count,
            scale=2.0 * product_scale / math.sqrt(total_points),
        ),
        "first_half",
        (
            shape((width, probe_count, row_count), jnp.float32),
            shape((size_of(FIRST_SUM), 1, packed_sums), jnp.float32),
            shape((width, count + EXTRA, row_count), jnp.bfloat16),
            shape((width, row_count, count + EXTRA), jnp.bfloat16),
            shape((width, probe_count, row_count), jnp.bfloat16),
        ),
        ahead,
        quad,
        pieces,
        pivot_all,
        pivot_here,
        scalars=1,
        flops=flops,
        exps=exps,
    )
    some = exchanged(spread, FIRST_SUM)
    sums = local(
        functools.partial(second_half_kernel, scale=product_scale),
        "second_half",
        shape((width, probe_count, row_count), jnp.float32),
        ahead,
        row_all,
        col_all,
        col_probe,
        first,
        scalars=1,
        flops=flops,
        exps=exps,
    )
    spread = local(
        sum_spread_kernel,
        "first_sum",
        shape((size_of(SECOND_SUM), 1, packed_sums), jnp.float32),
        some,
    )
    parts = local(
        join_kernel,
        "join",
        shape((width, probe_count, row_count + 2 * rank), jnp.float32),
        sums,
        exchanged(spread, SECOND_SUM),
    )
    product, projection, quadratic = local(
        functools.partial(finish_kernel, projection_scale=8.0 / math.sqrt(total_points)),
        "finish",
        (
            shape((probe_count, row_count), jnp.float32),
            shape((probe_count, rank), jnp.float32),
            shape((probe_count,), jnp.float32),
        ),
        exchanged(parts, "x"),
    )
    return product, projection, quadratic


def solution(mesh):
    fine = Mesh(mesh.devices.reshape(Y, ZLO, CORE, ZHI, X), ALL_AXES)
    split = P(None, ALL_AXES)
    return jax.shard_map(
        body,
        mesh=fine,
        in_specs=(split, split, P(), P(), P()),
        out_specs=(split, P(), P()),
        check_vma=False,
    )
```

```python
import functools
import math

import jax
import jax.numpy as jnp
from jax import lax
from jax.experimental import pallas as pl
from jax.experimental.pallas import tpu as pltpu
from jax.sharding import Mesh
from jax.sharding import PartitionSpec as P

Y, ZLO, CORE, ZHI, X = 8, 4, 2, 2, 4
GROUP_AXES = ("y", "zlo", "core")
ALL_AXES = ("y", "zlo", "core", "zhi", "x")
FIRST_SUM, SECOND_SUM = ("y", "core"), ("zlo", "zhi")
MAX_SHIFT = 31
EXTRA = 16
VMEM_LIMIT = 48 * 2**20


def size_of(axes):
    return lax.axis_size(axes)


def exchanged(x, axes):
    return lax.all_to_all(x, axes, 0, 0)


def from_partner(x, shift):
    groups, halves, width = size_of(GROUP_AXES), size_of("zhi"), size_of("x")
    pairs = []
    for group in range(groups):
        for half in range(halves):
            for place in range(width):
                way = 1 - 2 * ((place + group) % 2)
                source = (group + way * shift) % groups
                source = (source * halves + (half ^ place // 2)) * width + place
                pairs.append((source, (group * halves + half) * width + place))
    return lax.ppermute(x, ALL_AXES, pairs)


def local(
    kernel, name, out_shape, *args, scalars=0, flops=0, exps=0, scratch=(), space=pltpu.VMEM, room=VMEM_LIMIT
):
    moved = sum(math.prod(a.shape) * a.dtype.itemsize for a in args)
    specs = [pl.BlockSpec(memory_space=pltpu.SMEM)] * scalars
    specs += [pl.BlockSpec(memory_space=space)] * (len(args) - scalars)
    return pl.pallas_call(
        kernel,
        name=name,
        out_shape=out_shape,
        in_specs=specs,
        out_specs=jax.tree.map(lambda _: pl.BlockSpec(memory_space=pltpu.VMEM), out_shape),
        scratch_shapes=scratch,
        cost_estimate=pl.CostEstimate(flops=flops, bytes_accessed=moved, transcendentals=exps),
        compiler_params=pltpu.CompilerParams(vmem_limit_bytes=room),
    )(*args)


def extended(feat, ones_first):
    wide = feat.astype(jnp.float32)
    half = -0.5 * jnp.sum(wide * wide, axis=0, keepdims=True)
    high = half.astype(jnp.bfloat16).astype(jnp.float32)
    middle = (half - high).astype(jnp.bfloat16).astype(jnp.float32)
    low = half - high - middle
    row = lax.broadcasted_iota(jnp.int32, (EXTRA, feat.shape[1]), 0)
    ones, norm = (0, 3) if ones_first else (3, 0)
    rest = jnp.where((row >= ones) & (row < ones + 3), 1.0, 0.0)
    for offset, piece in enumerate((high, middle, low)):
        rest = jnp.where(row == norm + offset, piece, rest)
    return jnp.concatenate([feat, rest.astype(jnp.bfloat16)], axis=0)


def turned(x):
    return x.astype(jnp.float32).T.astype(jnp.bfloat16)


def prepare_kernel(feat_hbm, scale_hbm, probe_hbm, out_ref, feat_ref, scale_ref, probe_ref, done):
    copies = [
        pltpu.make_async_copy(source, target, done.at[index])
        for index, (source, target) in enumerate(
            ((feat_hbm, feat_ref), (scale_hbm, scale_ref), (probe_hbm, probe_ref))
        )
    ]
    for copy in copies:
        copy.start()
    for copy in copies:
        copy.wait()
    count = feat_ref.shape[0]
    row = lax.broadcasted_iota(jnp.int32, (count, count), 0)
    col = lax.broadcasted_iota(jnp.int32, (count, count), 1)
    spread = jnp.broadcast_to(scale_ref[...], (count, count))
    scale = jnp.sum(jnp.where(row == col, spread, 0.0), axis=1, keepdims=True)
    scaled = (feat_ref[...] * jnp.sqrt(scale)).astype(jnp.bfloat16)
    packed = jnp.concatenate([scaled, probe_ref[...]], axis=0)
    for copy in range(out_ref.shape[0]):
        out_ref[copy] = packed


def own_pivots_kernel(first_ref, packed_ref, pivot_ref, out_ref, other_ref):
    count, rank = out_ref.shape[1:]
    points = packed_ref.shape[2]
    point = lax.broadcasted_iota(jnp.int32, (points, rank), 0) + first_ref[0]
    mask = jnp.where(point == pivot_ref[...], 1.0, 0.0).astype(jnp.bfloat16)
    part = jnp.dot(packed_ref[0, :count], mask, preferred_element_type=jnp.float32)
    for target in (out_ref, other_ref):
        for copy in range(target.shape[0]):
            target[copy] = part.astype(jnp.bfloat16)


def sum_spread_kernel(in_ref, out_ref):
    total = in_ref[0].astype(jnp.float32)
    for peer in range(1, in_ref.shape[0]):
        total = total + in_ref[peer].astype(jnp.float32)
    for copy in range(out_ref.shape[0]):
        out_ref[copy] = total.astype(out_ref.dtype)


def pair_sum(row_all, col_all, col_probe, place, other):
    power = jnp.dot(col_all[other], row_all[place], preferred_element_type=jnp.float32)
    kernel = jnp.exp(power).astype(jnp.bfloat16)
    return jnp.dot(col_probe[other], kernel, preferred_element_type=jnp.float32)


def first_half_kernel(
    ahead_ref,
    row_ref,
    col_ref,
    pivot_ref,
    here_ref,
    sum_ref,
    out_ref,
    row_all,
    col_all,
    col_probe,
    *,
    count,
    scale,
):
    width, probes = row_ref.shape[0], sum_ref.shape[1]
    ahead = ahead_ref[0] == 1
    for place in range(width):
        row_all[place] = extended(row_ref[place, :count], True)
        col_all[place] = turned(extended(col_ref[place, :count], False))
        col_probe[place] = col_ref[place, count : count + probes]
    sum_ref[...] = jnp.zeros_like(sum_ref)

    def step(turn, carry):
        for part in range(2):
            place = jnp.where(ahead, 2 * turn + part, 2 + turn)
            first = jnp.where(ahead, 0, 2 * part)
            sum_ref[place] += pair_sum(row_all, col_all, col_probe, place, first) + pair_sum(
                row_all, col_all, col_probe, place, first + 1
            )
        return carry

    for turn in range(2):
        step(turn, 0)
    quad = jnp.zeros((probes, 1), jnp.float32)
    for place in range(width):
        row_probe = row_ref[place, count : count + probes].astype(jnp.float32)
        quad = quad + jnp.sum(row_probe * sum_ref[place], axis=1, keepdims=True)
    rank = pivot_ref.shape[2]
    pivot = pivot_ref[0].astype(jnp.float32)
    for peer in range(1, pivot_ref.shape[0]):
        pivot = pivot + pivot_ref[peer].astype(jnp.float32)
    pivot = turned(extended(pivot.astype(jnp.bfloat16), False))
    total = jnp.zeros((probes, rank), jnp.float32)
    for place in range(width):
        power = jnp.dot(pivot, row_all[place], preferred_element_type=jnp.float32)
        kernel = jnp.exp(power).astype(jnp.bfloat16)
        total = total + lax.dot_general(
            row_ref[place, count : count + probes],
            kernel,
            (((1,), (1,)), ((), ())),
            preferred_element_type=jnp.float32,
        )
    total = jnp.where(here_ref[...] != 0, total, 0.0)
    rows = [total[probe : probe + 1] for probe in range(probes)]
    row = lax.broadcasted_iota(jnp.int32, (probes, rank), 0)
    lane = lax.broadcasted_iota(jnp.int32, (probes, rank), 1)
    quad = jnp.broadcast_to(scale * quad, (probes, rank))
    rows.append(jnp.sum(jnp.where(row == lane, quad, 0.0), axis=0, keepdims=True))
    packed = jnp.concatenate(rows, axis=1)
    for copy in range(out_ref.shape[0]):
        out_ref[copy] = packed


def second_half_kernel(ahead_ref, row_all, col_all, col_probe, first_ref, sum_ref, *, scale):
    width = first_ref.shape[0]
    ahead = ahead_ref[0] == 1
    sum_ref[...] = first_ref[...]

    def step(turn, carry):
        for part in range(4):
            place = jnp.where(ahead, 2 * turn + part // 2, turn)
            other = jnp.where(ahead, 2 + part % 2, part)
            sum_ref[place] += pair_sum(row_all, col_all, col_probe, place, other)
        return carry

    lax.fori_loop(0, 2, step, 0)
    for place in range(width):
        sum_ref[place] = scale * sum_ref[place]


def join_kernel(sum_ref, total_ref, out_ref):
    width, probes, points = sum_ref.shape
    rank = (out_ref.shape[2] - points) // 2
    total = total_ref[0]
    for peer in range(1, total_ref.shape[0]):
        total = total + total_ref[peer]
    rows = [total[:, probe * rank : (probe + 1) * rank] for probe in range(probes)]
    last = jnp.broadcast_to(total[:, probes * rank :], (probes, rank))
    joined = jnp.concatenate([jnp.concatenate(rows, axis=0), last], axis=1)
    for place in range(width):
        out_ref[place, :, :points] = sum_ref[place]
        out_ref[place, :, points:] = joined


def finish_kernel(in_ref, product_ref, projection_ref, quadratic_ref, *, projection_scale):
    probes, points = product_ref.shape
    rank = projection_ref.shape[1]
    total = in_ref[0]
    for peer in range(1, in_ref.shape[0]):
        total = total + in_ref[peer]
    product_ref[...] = total[:, :points]
    projection_ref[...] = projection_scale * total[:, points : points + rank]
    quadratic_ref[...] = total[0, points + rank : points + rank + probes]


def body(features, probes, inverse_scales, round_index, pivots):
    count, row_count = features.shape
    probe_count, rank = probes.shape[0], pivots.shape[0]
    rows = count + probe_count
    width = size_of("x")
    block_points = row_count * size_of(("zhi", "x"))
    total_points = block_points * size_of(GROUP_AXES)
    shape = jax.ShapeDtypeStruct

    packed = local(
        prepare_kernel,
        "prepare",
        shape((width, rows, row_count), jnp.bfloat16),
        features,
        inverse_scales.reshape(1, count),
        probes,
        scratch=(
            pltpu.VMEM(features.shape, features.dtype),
            pltpu.VMEM((1, count), inverse_scales.dtype),
            pltpu.VMEM(probes.shape, probes.dtype),
            pltpu.SemaphoreType.DMA((3,)),
        ),
        space=pltpu.HBM,
        room=60 * 2**20,
    )
    quad = exchanged(packed, "x")

    first_point = (lax.axis_index(ALL_AXES) * row_count).astype(jnp.int32)
    pivot_row = pivots.reshape(1, rank)
    pivot_part, pivot_wide = local(
        own_pivots_kernel,
        "own_pivots",
        (
            shape((size_of(SECOND_SUM), count, rank), jnp.bfloat16),
            shape((size_of(FIRST_SUM), count, rank), jnp.bfloat16),
        ),
        first_point.reshape(1),
        packed,
        pivot_row,
        scalars=1,
        flops=2 * count * row_count * rank,
    )
    pivot_here = (pivot_row // row_count % width == lax.axis_index("x")).astype(jnp.int32)

    def fetch(shift):
        y_first = shift % 8 == 4 and shift < 16
        one, two = (FIRST_SUM, SECOND_SUM) if y_first else (SECOND_SUM, FIRST_SUM)

        def branch(data, part, wide):
            some = local(
                sum_spread_kernel,
                "pivot_sum",
                shape((size_of(two), count, rank), jnp.bfloat16),
                exchanged(wide if y_first else part, one),
            )
            pieces = from_partner(data, shift)
            some = exchanged(some, two)
            if y_first:
                spare = size_of(FIRST_SUM) - size_of(SECOND_SUM)
                some = jnp.pad(some, ((0, spare), (0, 0), (0, 0)))
            return pieces, some

        return branch

    pieces, pivot_all = lax.switch(
        round_index[0] - 1, [fetch(k) for k in range(1, MAX_SHIFT + 1)], quad, pivot_part, pivot_wide
    )

    product_scale = 8.0 / math.sqrt(block_points)
    flops = (width * row_count) ** 2 * (count + EXTRA + probe_count)
    exps = (width * row_count) ** 2 // 2
    ahead = ((lax.axis_index("x") + lax.axis_index(GROUP_AXES) + 1) % 2).astype(jnp.int32).reshape(1)
    packed_sums = (probe_count + 1) * rank
    first, spread, row_all, col_all, col_probe = local(
        functools.partial(
            first_half_kernel,
            count=count,
            scale=2.0 * product_scale / math.sqrt(total_points),
        ),
        "first_half",
        (
            shape((width, probe_count, row_count), jnp.float32),
            shape((size_of(FIRST_SUM), 1, packed_sums), jnp.float32),
            shape((width, count + EXTRA, row_count), jnp.bfloat16),
            shape((width, row_count, count + EXTRA), jnp.bfloat16),
            shape((width, probe_count, row_count), jnp.bfloat16),
        ),
        ahead,
        quad,
        pieces,
        pivot_all,
        pivot_here,
        scalars=1,
        flops=flops,
        exps=exps,
    )
    some = exchanged(spread, FIRST_SUM)
    sums = local(
        functools.partial(second_half_kernel, scale=product_scale),
        "second_half",
        shape((width, probe_count, row_count), jnp.float32),
        ahead,
        row_all,
        col_all,
        col_probe,
        first,
        scalars=1,
        flops=flops,
        exps=exps,
    )
    spread = local(
        sum_spread_kernel,
        "first_sum",
        shape((size_of(SECOND_SUM), 1, packed_sums), jnp.float32),
        some,
    )
    parts = local(
        join_kernel,
        "join",
        shape((width, probe_count, row_count + 2 * rank), jnp.float32),
        sums,
        exchanged(spread, SECOND_SUM),
    )
    product, projection, quadratic = local(
        functools.partial(finish_kernel, projection_scale=8.0 / math.sqrt(total_points)),
        "finish",
        (
            shape((probe_count, row_count), jnp.float32),
            shape((probe_count, rank), jnp.float32),
            shape((probe_count,), jnp.float32),
        ),
        exchanged(parts, "x"),
    )
    return product, projection, quadratic


def solution(mesh):
    fine = Mesh(mesh.devices.reshape(Y, ZLO, CORE, ZHI, X), ALL_AXES)
    split = P(None, ALL_AXES)
    return jax.shard_map(
        body,
        mesh=fine,
        in_specs=(split, split, P(), P(), P()),
        out_specs=(split, P(), P()),
        check_vma=False,
    )
```
